32 devices in a mesh: row: 4 (over y, core), col: 8 (over z, x).
Axes of the slice: x: 2, y: 2, z: 4, core: 2. Of those that a mesh axis runs over, the one named last changes fastest.
Arguments:
- forward_head: bfloat16 [4, 2048, 1000], P(None, 'col'), may hold values from -6 to 6
- forward_tail: bfloat16 [57344, 1000], P(('col', 'row')), may hold values from -6 to 6
- forward_inverse: bfloat16 [4, 2048, 2048], P(None, 'col', 'row'), may hold values from -1.5 to 1.5, as said below
- forward_coupling: bfloat16 [6, 2048, 2048], P(None, 'row', 'col'), may hold values from -0.078125 to 0.078125
- forward_slab: bfloat16 [4, 2048, 57344], P(None, 'row', 'col'), may hold values from -0.0625 to 0.0625
- backward_head: bfloat16 [4, 2048, 1000], P(None, 'row'), may hold values from -6 to 6
- backward_tail: bfloat16 [57344, 1000], P(('row', 'col')), may hold values from -6 to 6
- backward_inverse: bfloat16 [4, 2048, 2048], P(None, 'col', 'row'), may hold values from -1.5 to 1.5, as said below
- backward_coupling: bfloat16 [6, 2048, 2048], P(None, 'row', 'col'), may hold values from -0.078125 to 0.078125
- backward_slab: bfloat16 [57344, 4, 2048], P('row', None, 'col'), may hold values from -0.0625 to 0.0625
Outputs:
- lower_head: bfloat16 [4, 2048, 1000], P(None, 'row')
- lower_tail: bfloat16 [57344, 1000], P(('col', 'row'))
- upper_head: bfloat16 [4, 2048, 1000], P(None, 'col')
- upper_tail: bfloat16 [57344, 1000], P(('row', 'col'))
The draws below stay inside these ranges and needn't reach their ends.
Inputs may be any that keep to these rules, and one draw needn't show every extreme that they name: Each block of forward_inverse is upper triangular with diagonal entries of magnitude 0.5 to 1.5. Each block of backward_inverse is upper triangular with diagonal entries of magnitude 0.5 to 1.5.
All inputs are finite; a program needn't handle non-finite values.
Results may differ from the reference program's by a relative error of at most 0.03.
Values may be sent and summed in bfloat16 or wider, within the bound.
A program may use at most 192 MiB of HBM per device.

```python
import jax
import jax.numpy as jnp
from jax import lax

K = 1000
PANEL = 2048
NP = 4
NTAIL = 57344
N_ROW = 4
N_COL = 8


def upper_inverse(key):
    key_spread, key_size, key_sign = jax.random.split(key, 3)
    spread = jnp.clip(jax.random.normal(key_spread, (NP, PANEL, PANEL), jnp.float32), -4.0, 4.0)
    positions = jnp.arange(PANEL)
    upper = (positions[:, None] < positions[None, :]).astype(jnp.float32)
    identity = (positions[:, None] == positions[None, :]).astype(jnp.float32)
    magnitude = jax.random.uniform(key_size, (NP, PANEL), jnp.float32, 0.5, 1.5)
    signs = jnp.where(jax.random.bernoulli(key_sign, 0.5, (NP, PANEL)), 1.0, -1.0)
    diagonal = identity[None, :, :] * (magnitude * signs)[:, None, :]
    result = spread * upper[None, :, :] / jnp.sqrt(jnp.float32(PANEL)) + diagonal
    return result.astype(jnp.bfloat16)


def draw_forward_inverse(key, part):
    return upper_inverse(jax.random.fold_in(key, 11))


def draw_backward_inverse(key, part):
    return upper_inverse(jax.random.fold_in(key, 23))


def level_of(key, extent, pieces, least, largest):
    def one(dim, shards_of):
        steps = jax.random.uniform(jax.random.fold_in(jax.random.fold_in(key, 6), dim), (shards_of,), jnp.float32, least / len(pieces), largest / len(pieces))
        return jnp.repeat(jnp.exp(steps), extent[dim] // shards_of).reshape((-1,) + (1,) * (len(extent) - dim - 1))

    gain = one(*pieces[0])
    for cut in pieces[1:]:
        gain = gain * one(*cut)
    return gain


def normal_values(key, shape, scale, reach, pieces=(), held_as=jnp.bfloat16):
    drawn = jax.random.normal(key, shape, jnp.float32) * scale
    if len(pieces) > 0:
        drawn = level_of(key, shape, pieces, -0.22, 0.18) * drawn
    return jnp.clip(drawn, min=-reach, max=reach).astype(held_as)


def setup_inputs(seed: int = 0) -> dict:
    key_of = jax.random.split(jax.random.key(seed), 11)
    return {
        "forward_head": normal_values(key_of[0], (NP, PANEL, K), 1.0, 6.0, ((1, 8),)),
        "forward_tail": normal_values(key_of[1], (NTAIL, K), 1.0, 6.0, ((0, 32),)),
        "forward_inverse": draw_forward_inverse(jax.random.fold_in(key_of[10], 71), 0),
        "forward_coupling": normal_values(key_of[3], (NP * (NP - 1) // 2, PANEL, PANEL), ((NP - 1) * PANEL) ** -0.5, 0.078125, ((1, 4), (2, 8))),
        "forward_slab": normal_values(key_of[4], (NP, PANEL, NTAIL), (NP * PANEL) ** -0.5, 0.0625, ((1, 4), (2, 8))),
        "backward_head": normal_values(key_of[5], (NP, PANEL, K), 1.0, 6.0, ((1, 4),)),
        "backward_tail": normal_values(key_of[6], (NTAIL, K), 1.0, 6.0, ((0, 32),)),
        "backward_inverse": draw_backward_inverse(jax.random.fold_in(key_of[10], 71), 0),
        "backward_coupling": normal_values(key_of[8], (NP * (NP - 1) // 2, PANEL, PANEL), ((NP - 1) * PANEL) ** -0.5, 0.078125, ((1, 4), (2, 8))),
        "backward_slab": normal_values(key_of[9], (NTAIL, NP, PANEL), (NP * PANEL) ** -0.5, 0.0625, ((0, 4), (2, 8))),
    }


def round_trip(value):
    return lax.optimization_barrier(value.astype(jnp.bfloat16)).astype(jnp.float32)


def reference(forward_head, forward_tail, forward_inverse, forward_coupling, forward_slab, backward_head, backward_tail, backward_inverse, backward_coupling, backward_slab):
    lower_list = []
    for panel_index in range(NP):
        if panel_index == 0:
            adjusted = forward_head[0]
        else:
            summed = jnp.zeros((PANEL, K), jnp.float32)
            for earlier in range(panel_index):
                block = forward_coupling[panel_index * (panel_index - 1) // 2 + earlier]
                summed = summed + jnp.dot(block.T, lower_list[earlier], preferred_element_type=jnp.float32)
            adjusted = (forward_head[panel_index].astype(jnp.float32) - summed).astype(jnp.bfloat16)
        lower_list.append(jnp.dot(forward_inverse[panel_index].T, adjusted, preferred_element_type=jnp.float32).astype(jnp.bfloat16))
    lower_head = jnp.stack(lower_list)
    panel_rows = PANEL // N_ROW
    accumulated = jnp.zeros((NTAIL, K), jnp.float32)
    for group in range(N_ROW):
        slab_piece = forward_slab[:, group * panel_rows:(group + 1) * panel_rows, :].reshape(NP * panel_rows, NTAIL)
        panel_piece = lower_head[:, group * panel_rows:(group + 1) * panel_rows, :].reshape(NP * panel_rows, K)
        partial_value = jnp.dot(slab_piece.T, panel_piece, preferred_element_type=jnp.float32)
        accumulated = accumulated + round_trip(partial_value)
    lower_tail = (forward_tail.astype(jnp.float32) - accumulated).astype(jnp.bfloat16)

    upper_list = [None] * NP
    for panel_index in reversed(range(NP)):
        if panel_index == NP - 1:
            shifted = backward_head[panel_index]
        else:
            summed = jnp.zeros((PANEL, K), jnp.float32)
            for later_panel in range(panel_index + 1, NP):
                block = backward_coupling[later_panel * (later_panel - 1) // 2 + panel_index]
                summed = summed + jnp.dot(block, upper_list[later_panel], preferred_element_type=jnp.float32)
            shifted = (backward_head[panel_index].astype(jnp.float32) - summed).astype(jnp.bfloat16)
        upper_list[panel_index] = jnp.dot(backward_inverse[panel_index], shifted, preferred_element_type=jnp.float32).astype(jnp.bfloat16)
    upper_head = jnp.stack(upper_list)
    panel_cols = PANEL // N_COL
    gathered_sum = jnp.zeros((NTAIL, K), jnp.float32)
    for group in range(N_COL):
        slab_piece = backward_slab[:, :, group * panel_cols:(group + 1) * panel_cols].reshape(NTAIL, NP * panel_cols)
        panel_piece = upper_head[:, group * panel_cols:(group + 1) * panel_cols, :].reshape(NP * panel_cols, K)
        partial_value = jnp.dot(slab_piece, panel_piece, preferred_element_type=jnp.float32)
        gathered_sum = gathered_sum + round_trip(partial_value)
    upper_tail = (backward_tail.astype(jnp.float32) - gathered_sum).astype(jnp.bfloat16)
    return (lower_head, lower_tail, upper_head, upper_tail)
```

```python
import functools

import jax
import jax.numpy as jnp
from jax import lax
from jax.experimental import pallas as pl
from jax.experimental.pallas import tpu as pltpu
from jax.sharding import PartitionSpec as P

NZ = 4
MESH = pl.DeviceIdType.MESH


def add_rows(dst, src, rows, step):
    def body(i, carry):
        at = pl.ds(pl.multiple_of(i * step, step), step)
        dst[at, :] = (dst[at, :].astype(jnp.float32) + src[at, :].astype(jnp.float32)).astype(
            jnp.bfloat16
        )
        return carry

    lax.fori_loop(0, rows // step, body, 0)


def col_scatter_kernel(
    nx, chunk, part, tail, out, from_x, from_z, own, x_send, x_recv, z_send, z_recv, own_sem
):
    rows = tail.shape[0]
    count = rows // chunk
    col = lax.axis_index("col")
    z, x = col // nx, col % nx
    step = 64

    barrier = pltpu.get_barrier_semaphore()
    for i in range(1, nx):
        pl.semaphore_signal(
            barrier, inc=1, device_id={"col": z * nx + (x + i) % nx}, device_id_type=MESH
        )
    for j in range(1, NZ):
        pl.semaphore_signal(
            barrier, inc=1, device_id={"col": (z + j) % NZ * nx + x}, device_id_type=MESH
        )
    pl.semaphore_wait(barrier, nx - 1 + NZ - 1)

    units = [(k, j) for k in range(count) for j in range(NZ)]

    def piece(k, j, to_x):
        return part.at[pl.ds(pl.multiple_of(((z + 1 + j) % NZ * nx + to_x) * rows + k * chunk, 64), chunk), :]

    def x_copy(u, i):
        k, j = units[u]
        to_x = (x + i) % nx
        return pltpu.make_async_remote_copy(
            src_ref=piece(k, j, to_x),
            dst_ref=from_x.at[i - 1, u],
            send_sem=x_send.at[i - 1, u],
            recv_sem=x_recv.at[i - 1, u],
            device_id={"col": z * nx + to_x},
            device_id_type=MESH,
        )

    def own_copy(u):
        k, j = units[u]
        return pltpu.make_async_copy(piece(k, j, x), own.at[u % 2], own_sem.at[u % 2])

    def z_copy(u):
        k, j = units[u]
        return pltpu.make_async_remote_copy(
            src_ref=from_x.at[0, u],
            dst_ref=from_z.at[j, k],
            send_sem=z_send.at[j, k],
            recv_sem=z_recv.at[j, k],
            device_id={"col": (z + 1 + j) % NZ * nx + x},
            device_id_type=MESH,
        )

    ahead = 4
    for u in range(min(ahead, len(units))):
        for i in range(1, nx):
            x_copy(u, i).start()
    own_copy(0).start()

    def finish(k):
        for j in range(NZ - 1):
            z_copy(k * NZ + j).wait_recv()
        mine = from_x.at[0, k * NZ + NZ - 1]

        def body(i, carry):
            at = pl.ds(pl.multiple_of(i * step, step), step)
            total = mine[at, :].astype(jnp.float32)
            for j in range(NZ - 1):
                total = total + from_z[j, k, at, :].astype(jnp.float32)
            here = pl.ds(pl.multiple_of(k * chunk + i * step, step), step)
            out[here, :] = (tail[here, :].astype(jnp.float32) - total).astype(jnp.bfloat16)
            return carry

        lax.fori_loop(0, chunk // step, body, 0)

    for u, (k, j) in enumerate(units):
        if u + 1 < len(units):
            own_copy(u + 1).start()
        own_copy(u).wait()
        for i in range(1, nx):
            x_copy(u, i).wait_recv()
        if u + ahead < len(units):
            for i in range(1, nx):
                x_copy(u + ahead, i).start()
        add_rows(from_x.at[0, u], own.at[u % 2], chunk, step)
        for i in range(2, nx):
            add_rows(from_x.at[0, u], from_x.at[i - 1, u], chunk, step)
        if j < NZ - 1:
            z_copy(u).start()
        elif k >= 1:
            finish(k - 1)
    finish(count - 1)
    for u, (k, j) in enumerate(units):
        for i in range(1, nx):
            x_copy(u, i).wait_send()
        if j < NZ - 1:
            z_copy(u).wait_send()


def col_scatter(part, tail, ncol):
    nx = ncol // NZ
    rows, classes = tail.shape
    chunk = 448
    count = rows // chunk
    vmem = pl.BlockSpec(memory_space=pltpu.VMEM)
    return pl.pallas_call(
        functools.partial(col_scatter_kernel, nx, chunk),
        out_shape=jax.ShapeDtypeStruct(tail.shape, jnp.bfloat16),
        in_specs=[pl.BlockSpec(memory_space=pl.ANY), vmem],
        out_specs=vmem,
        scratch_shapes=[
            pltpu.VMEM((nx - 1, count * NZ, chunk, classes), jnp.bfloat16),
            pltpu.VMEM((NZ - 1, count, chunk, classes), jnp.bfloat16),
            pltpu.VMEM((2, chunk, classes), jnp.bfloat16),
            pltpu.SemaphoreType.DMA((nx - 1, count * NZ)),
            pltpu.SemaphoreType.DMA((nx - 1, count * NZ)),
            pltpu.SemaphoreType.DMA((NZ - 1, count)),
            pltpu.SemaphoreType.DMA((NZ - 1, count)),
            pltpu.SemaphoreType.DMA((2,)),
        ],
        compiler_params=pltpu.CompilerParams(
            collective_id=1, has_side_effects=True, vmem_limit_bytes=50 * 1024 * 1024
        ),
        cost_estimate=pl.CostEstimate(
            flops=10**9, bytes_accessed=part.size * 16, transcendentals=0
        ),
        name="col_scatter",
    )(part, tail)


def reduce_row(value):
    return lax.psum(value.astype(jnp.bfloat16), "row").astype(jnp.float32)


def reduce_col(value):
    return lax.psum(value.astype(jnp.bfloat16), "col").astype(jnp.float32)


def leading_dot(left, right):
    return lax.dot_general(
        left, right, (((0,), (0,)), ((), ())), preferred_element_type=jnp.float32
    )


def local(
    forward_head,
    forward_tail,
    forward_inverse,
    forward_coupling,
    forward_slab,
    backward_head,
    backward_tail,
    backward_inverse,
    backward_coupling,
    backward_slab,
):
    classes = forward_head.shape[2]
    panels = forward_head.shape[0]
    lower_list = []
    for panel_index in range(panels):
        if panel_index == 0:
            adjusted = forward_head[0]
        else:
            summed = leading_dot(
                forward_coupling[panel_index * (panel_index - 1) // 2], lower_list[0]
            )
            for earlier in range(1, panel_index):
                summed = summed + leading_dot(
                    forward_coupling[panel_index * (panel_index - 1) // 2 + earlier],
                    lower_list[earlier],
                )
            coupling = reduce_row(summed)
            adjusted = (forward_head[panel_index].astype(jnp.float32) - coupling).astype(
                jnp.bfloat16
            )
        lower_list.append(
            reduce_col(leading_dot(forward_inverse[panel_index], adjusted)).astype(jnp.bfloat16)
        )
    lower_head = jnp.stack(lower_list)
    panel_rows = lower_head.shape[1]
    flat_lower = lower_head.reshape(panels * panel_rows, classes)
    flat_slab = forward_slab.reshape(panels * panel_rows, forward_slab.shape[2])
    lower_update = lax.psum_scatter(
        leading_dot(flat_slab, flat_lower).astype(jnp.bfloat16),
        "row",
        scatter_dimension=0,
        tiled=True,
    ).astype(jnp.float32)
    lower_tail = (forward_tail.astype(jnp.float32) - lower_update).astype(jnp.bfloat16)
    upper_list = [None] * panels
    for panel_index in reversed(range(panels)):
        if panel_index == panels - 1:
            shifted = backward_head[panel_index]
        else:
            summed = None
            for later_panel in range(panel_index + 1, panels):
                block = backward_coupling[later_panel * (later_panel - 1) // 2 + panel_index]
                product = jnp.dot(
                    block, upper_list[later_panel], preferred_element_type=jnp.float32
                )
                summed = product if summed is None else summed + product
            pulled = reduce_col(summed)
            shifted = (backward_head[panel_index].astype(jnp.float32) - pulled).astype(jnp.bfloat16)
        upper_list[panel_index] = reduce_row(
            jnp.dot(backward_inverse[panel_index], shifted, preferred_element_type=jnp.float32)
        ).astype(jnp.bfloat16)
    upper_head = jnp.stack(upper_list)
    panel_cols = upper_head.shape[1]
    flat_back = backward_slab.reshape(backward_slab.shape[0], panels * panel_cols)
    flat_upper = upper_head.reshape(panels * panel_cols, classes)
    part = jnp.dot(flat_back, flat_upper, preferred_element_type=jnp.float32).astype(jnp.bfloat16)
    upper_tail = col_scatter(part, backward_tail, lax.axis_size("col"))
    return (lower_head, lower_tail, upper_head, upper_tail)


def solution(mesh):
    in_specs = (
        P(None, "col", None),
        P(("col", "row"), None),
        P(None, "col", "row"),
        P(None, "row", "col"),
        P(None, "row", "col"),
        P(None, "row", None),
        P(("row", "col"), None),
        P(None, "col", "row"),
        P(None, "row", "col"),
        P("row", None, "col"),
    )
    out_specs = (
        P(None, "row", None),
        P(("col", "row"), None),
        P(None, "col", None),
        P(("row", "col"), None),
    )
    return jax.shard_map(local, mesh=mesh, in_specs=in_specs, out_specs=out_specs, check_vma=False)
```

```python
import functools

import jax
import jax.numpy as jnp
from jax import lax
from jax.experimental import pallas as pl
from jax.experimental.pallas import tpu as pltpu
from jax.sharding import PartitionSpec as P

NZ = 4
MESH = pl.DeviceIdType.MESH


def add_rows(dst, src, rows, step):
    def body(i, carry):
        at = pl.ds(pl.multiple_of(i * step, step), step)
        dst[at, :] = (dst[at, :].astype(jnp.float32) + src[at, :].astype(jnp.float32)).astype(
            jnp.bfloat16
        )
        return carry

    lax.fori_loop(0, rows // step, body, 0)


def col_scatter_kernel(
    nx, chunk, part, tail, out, from_x, from_z, own, x_send, x_recv, z_send, z_recv, own_sem
):
    rows = tail.shape[0]
    count = rows // chunk
    col = lax.axis_index("col")
    z, x = col // nx, col % nx
    step = 64

    barrier = pltpu.get_barrier_semaphore()
    for i in range(1, nx):
        pl.semaphore_signal(
            barrier, inc=1, device_id={"col": z * nx + (x + i) % nx}, device_id_type=MESH
        )
    for j in range(1, NZ):
        pl.semaphore_signal(
            barrier, inc=1, device_id={"col": (z + j) % NZ * nx + x}, device_id_type=MESH
        )
    pl.semaphore_wait(barrier, nx - 1 + NZ - 1)

    units = [(k, j) for k in range(count) for j in range(NZ)]

    def piece(k, j, to_x):
        return part.at[pl.ds(pl.multiple_of(((z + 1 + j) % NZ * nx + to_x) * rows + k * chunk, 64), chunk), :]

    def x_copy(u, i):
        k, j = units[u]
        to_x = (x + i) % nx
        return pltpu.make_async_remote_copy(
            src_ref=piece(k, j, to_x),
            dst_ref=from_x.at[i - 1, u],
            send_sem=x_send.at[i - 1, u],
            recv_sem=x_recv.at[i - 1, u],
            device_id={"col": z * nx + to_x},
            device_id_type=MESH,
        )

    def own_copy(u):
        k, j = units[u]
        return pltpu.make_async_copy(piece(k, j, x), own.at[u % 2], own_sem.at[u % 2])

    def z_copy(u):
        k, j = units[u]
        return pltpu.make_async_remote_copy(
            src_ref=from_x.at[0, u],
            dst_ref=from_z.at[j, k],
            send_sem=z_send.at[j, k],
            recv_sem=z_recv.at[j, k],
            device_id={"col": (z + 1 + j) % NZ * nx + x},
            device_id_type=MESH,
        )

    ahead = 4
    for u in range(min(ahead, len(units))):
        for i in range(1, nx):
            x_copy(u, i).start()
    own_copy(0).start()

    def finish(k):
        for j in range(NZ - 1):
            z_copy(k * NZ + j).wait_recv()
        mine = from_x.at[0, k * NZ + NZ - 1]

        def body(i, carry):
            at = pl.ds(pl.multiple_of(i * step, step), step)
            total = mine[at, :].astype(jnp.float32)
            for j in range(NZ - 1):
                total = total + from_z[j, k, at, :].astype(jnp.float32)
            here = pl.ds(pl.multiple_of(k * chunk + i * step, step), step)
            out[here, :] = (tail[here, :].astype(jnp.float32) - total).astype(jnp.bfloat16)
            return carry

        lax.fori_loop(0, chunk // step, body, 0)

    for u, (k, j) in enumerate(units):
        if u + 1 < len(units):
            own_copy(u + 1).start()
        own_copy(u).wait()
        for i in range(1, nx):
            x_copy(u, i).wait_recv()
        if u + ahead < len(units):
            for i in range(1, nx):
                x_copy(u + ahead, i).start()
        add_rows(from_x.at[0, u], own.at[u % 2], chunk, step)
        for i in range(2, nx):
            add_rows(from_x.at[0, u], from_x.at[i - 1, u], chunk, step)
        if j < NZ - 1:
            z_copy(u).start()
        elif k >= 1:
            finish(k - 1)
    finish(count - 1)
    for u, (k, j) in enumerate(units):
        for i in range(1, nx):
            x_copy(u, i).wait_send()
        if j < NZ - 1:
            z_copy(u).wait_send()


def col_scatter(part, tail, ncol):
    nx = ncol // NZ
    rows, classes = tail.shape
    chunk = 448
    count = rows // chunk
    vmem = pl.BlockSpec(memory_space=pltpu.VMEM)
    return pl.pallas_call(
        functools.partial(col_scatter_kernel, nx, chunk),
        out_shape=jax.ShapeDtypeStruct(tail.shape, jnp.bfloat16),
        in_specs=[pl.BlockSpec(memory_space=pl.ANY), vmem],
        out_specs=vmem,
        scratch_shapes=[
            pltpu.VMEM((nx - 1, count * NZ, chunk, classes), jnp.bfloat16),
            pltpu.VMEM((NZ - 1, count, chunk, classes), jnp.bfloat16),
            pltpu.VMEM((2, chunk, classes), jnp.bfloat16),
            pltpu.SemaphoreType.DMA((nx - 1, count * NZ)),
            pltpu.SemaphoreType.DMA((nx - 1, count * NZ)),
            pltpu.SemaphoreType.DMA((NZ - 1, count)),
            pltpu.SemaphoreType.DMA((NZ - 1, count)),
            pltpu.SemaphoreType.DMA((2,)),
        ],
        compiler_params=pltpu.CompilerParams(
            collective_id=1, has_side_effects=True, vmem_limit_bytes=50 * 1024 * 1024
        ),
        cost_estimate=pl.CostEstimate(
            flops=10**9, bytes_accessed=part.size * 16, transcendentals=0
        ),
        name="col_scatter",
    )(part, tail)


def col_reduce_kernel(
    nx, value, out, from_x, from_z, full, x_send, x_recv, z_send, z_recv, gx_send, gx_recv, gz_send, gz_recv
):
    rows = full.shape[1]
    col = lax.axis_index("col")
    z, x = col // nx, col % nx
    step = 16

    barrier = pltpu.get_barrier_semaphore()
    for i in range(1, nx):
        pl.semaphore_signal(
            barrier, inc=1, device_id={"col": z * nx + (x + i) % nx}, device_id_type=MESH
        )
    for j in range(1, NZ):
        pl.semaphore_signal(
            barrier, inc=1, device_id={"col": (z + j) % NZ * nx + x}, device_id_type=MESH
        )
    pl.semaphore_wait(barrier, nx - 1 + NZ - 1)

    def piece(j, to_x):
        start = ((z + 1 + j) % NZ * nx + to_x) * rows
        return value.at[pl.ds(pl.multiple_of(start, 16), rows), :]

    def remote(src, dst, send, recv, target):
        return pltpu.make_async_remote_copy(
            src_ref=src,
            dst_ref=dst,
            send_sem=send,
            recv_sem=recv,
            device_id={"col": target},
            device_id_type=MESH,
        )

    def x_copy(j, i):
        to_x = (x + i) % nx
        return remote(
            piece(j, to_x), from_x.at[i - 1, j], x_send.at[i - 1, j], x_recv.at[i - 1, j], z * nx + to_x
        )

    def z_copy(j):
        return remote(
            from_x.at[0, j], from_z.at[j], z_send.at[j], z_recv.at[j], (z + 1 + j) % NZ * nx + x
        )

    def gather_z(j):
        return remote(
            full.at[col], full.at[col], gz_send.at[j], gz_recv.at[j], (z + 1 + j) % NZ * nx + x
        )

    def gather_x(j, i, of_x):
        block = full.at[(z + NZ - 1 - j) % NZ * nx + of_x]
        return remote(
            block, block, gx_send.at[i - 1, j], gx_recv.at[i - 1, j], z * nx + (x + i) % nx
        )

    for j in range(NZ):
        for i in range(1, nx):
            x_copy(j, i).start()
    for j in range(NZ):
        for i in range(1, nx):
            x_copy(j, i).wait_recv()
        add_rows(from_x.at[0, j], piece(j, x), rows, step)
        for i in range(2, nx):
            add_rows(from_x.at[0, j], from_x.at[i - 1, j], rows, step)
        if j < NZ - 1:
            z_copy(j).start()
    for j in range(NZ - 1):
        z_copy(j).wait_recv()

    def body(i, carry):
        at = pl.ds(pl.multiple_of(i * step, step), step)
        total = from_x[0, NZ - 1, at, :].astype(jnp.float32)
        for j in range(NZ - 1):
            total = total + from_z[j, at, :].astype(jnp.float32)
        full[col, at, :] = total.astype(jnp.bfloat16)
        return carry

    lax.fori_loop(0, rows // step, body, 0)
    for j in range(NZ - 1):
        gather_z(j).start()
    for i in range(1, nx):
        gather_x(NZ - 1, i, x).start()
    for j in range(NZ - 1):
        block = full.at[(z + NZ - 1 - j) % NZ * nx + x]
        remote(
            block, block, gz_send.at[j], gz_recv.at[j], (z + 1 + j) % NZ * nx + x
        ).wait_recv()
        for i in range(1, nx):
            gather_x(j, i, x).start()
    for j in range(NZ):
        for i in range(1, nx):
            gather_x(j, i, (x + nx - i) % nx).wait_recv()
    for j in range(NZ):
        for i in range(1, nx):
            x_copy(j, i).wait_send()
            gather_x(j, i, x).wait_send()
        if j < NZ - 1:
            z_copy(j).wait_send()
            gather_z(j).wait_send()

    def emit(b, carry):
        out[pl.ds(pl.multiple_of(b * rows, 16), rows), :] = full[b]
        return carry

    lax.fori_loop(0, full.shape[0], emit, 0)


def col_reduce(value, ident):
    ncol = lax.axis_size("col")
    nx = ncol // NZ
    rows, classes = value.shape[0] // ncol, value.shape[1]
    vmem = pl.BlockSpec(memory_space=pltpu.VMEM)
    dma = pltpu.SemaphoreType.DMA
    return pl.pallas_call(
        functools.partial(col_reduce_kernel, nx),
        out_shape=jax.ShapeDtypeStruct(value.shape, jnp.bfloat16),
        in_specs=[vmem],
        out_specs=vmem,
        scratch_shapes=[
            pltpu.VMEM((nx - 1, NZ, rows, classes), jnp.bfloat16),
            pltpu.VMEM((NZ - 1, rows, classes), jnp.bfloat16),
            pltpu.VMEM((ncol, rows, classes), jnp.bfloat16),
            dma((nx - 1, NZ)),
            dma((nx - 1, NZ)),
            dma((NZ - 1,)),
            dma((NZ - 1,)),
            dma((nx - 1, NZ)),
            dma((nx - 1, NZ)),
            dma((NZ - 1,)),
            dma((NZ - 1,)),
        ],
        compiler_params=pltpu.CompilerParams(
            collective_id=ident, has_side_effects=True, vmem_limit_bytes=24 * 1024 * 1024
        ),
        cost_estimate=pl.CostEstimate(
            flops=10**7, bytes_accessed=value.size * 16, transcendentals=0
        ),
        name="col_reduce",
    )(value)


def reduce_row(value):
    return lax.psum(value.astype(jnp.bfloat16), "row").astype(jnp.float32)


def leading_dot(left, right):
    return lax.dot_general(
        left, right, (((0,), (0,)), ((), ())), preferred_element_type=jnp.float32
    )


def local(
    forward_head,
    forward_tail,
    forward_inverse,
    forward_coupling,
    forward_slab,
    backward_head,
    backward_tail,
    backward_inverse,
    backward_coupling,
    backward_slab,
):
    classes = forward_head.shape[2]
    panels = forward_head.shape[0]
    bf16, f32 = jnp.bfloat16, jnp.float32
    last = panels - 1
    lower_list = [col_reduce(leading_dot(forward_inverse[0], forward_head[0]).astype(bf16), 2)]
    upper_list = [None] * panels
    upper_list[last] = reduce_row(
        jnp.dot(backward_inverse[last], backward_head[last], preferred_element_type=f32)
    ).astype(bf16)
    for stage in range(1, panels):
        summed = None
        for earlier in range(stage):
            product = leading_dot(
                forward_coupling[stage * (stage - 1) // 2 + earlier], lower_list[earlier]
            )
            summed = product if summed is None else summed + product
        adjusted = (forward_head[stage].astype(f32) - reduce_row(summed)).astype(bf16)
        back = last - stage
        pulled = None
        for later in range(back + 1, panels):
            product = jnp.dot(
                backward_coupling[later * (later - 1) // 2 + back],
                upper_list[later],
                preferred_element_type=f32,
            )
            pulled = product if pulled is None else pulled + product
        lower = leading_dot(forward_inverse[stage], adjusted).astype(bf16)
        both = col_reduce(jnp.concatenate([lower, pulled.astype(bf16)]), 3)
        lower_list.append(both[: lower.shape[0]])
        shifted = (backward_head[back].astype(f32) - both[lower.shape[0] :].astype(f32)).astype(bf16)
        upper_list[back] = reduce_row(
            jnp.dot(backward_inverse[back], shifted, preferred_element_type=f32)
        ).astype(bf16)
    lower_head = jnp.stack(lower_list)
    panel_rows = lower_head.shape[1]
    flat_lower = lower_head.reshape(panels * panel_rows, classes)
    flat_slab = forward_slab.reshape(panels * panel_rows, forward_slab.shape[2])
    lower_update = lax.psum_scatter(
        leading_dot(flat_slab, flat_lower).astype(jnp.bfloat16),
        "row",
        scatter_dimension=0,
        tiled=True,
    ).astype(jnp.float32)
    lower_tail = (forward_tail.astype(jnp.float32) - lower_update).astype(jnp.bfloat16)
    upper_head = jnp.stack(upper_list)
    panel_cols = upper_head.shape[1]
    flat_back = backward_slab.reshape(backward_slab.shape[0], panels * panel_cols)
    flat_upper = upper_head.reshape(panels * panel_cols, classes)
    part = jnp.dot(flat_back, flat_upper, preferred_element_type=jnp.float32).astype(jnp.bfloat16)
    upper_tail = col_scatter(part, backward_tail, lax.axis_size("col"))
    return (lower_head, lower_tail, upper_head, upper_tail)


def solution(mesh):
    in_specs = (
        P(None, "col", None),
        P(("col", "row"), None),
        P(None, "col", "row"),
        P(None, "row", "col"),
        P(None, "row", "col"),
        P(None, "row", None),
        P(("row", "col"), None),
        P(None, "col", "row"),
        P(None, "row", "col"),
        P("row", None, "col"),
    )
    out_specs = (
        P(None, "row", None),
        P(("col", "row"), None),
        P(None, "col", None),
        P(("row", "col"), None),
    )
    return jax.shard_map(local, mesh=mesh, in_specs=in_specs, out_specs=out_specs, check_vma=False)
```
